256 devices in a mesh: row: 128 (over y_lo, z, x, core), col: 2 (over y_hi).
Axes of the slice: x: 4, y: 4 (y_hi: 2, y_lo: 2; y = y_hi * 2 + y_lo), z: 8, core: 2. Of those that a mesh axis runs over, the one named last changes fastest.
Arguments:
- vectors: float32 [196608, 2048], P('row', 'col'), may hold values from -6 to 6
- reflectors: bfloat16 [2, 196608, 128], P('col', 'row'), may hold values from -6 to 6
- factors: bfloat16 [2, 128, 128], P('col'), may hold values from -1.804027e-05 to 0.000200336686, as said below
Outputs:
- transformed: float32 [196608, 2048], P('row', 'col')
The draws below stay inside these ranges and needn't reach their ends.
Inputs may be any that keep to these rules, and one draw needn't show every extreme that they name: Each factors[b] is upper triangular with a positive diagonal.
All inputs are finite; a program needn't handle non-finite values.
Results may differ from the reference program's by a relative error of at most 0.0003.
Values may be sent and summed in bfloat16 or wider, within the bound.
A program may use at most 64 MiB of HBM per device.

```python
import jax
import jax.numpy as jnp
from jax import lax

NB = 128
M = 2048
N = 196608


def draw_factors(key, part):
    key = jax.random.fold_in(key, 7)
    key_diag, key_off = jax.random.split(key)
    diag_vals = jax.random.uniform(key_diag, (2, NB), jnp.float32, 0.5, 2.0)
    off_vals = jnp.clip(jax.random.normal(key_off, (2, NB, NB), jnp.float32), -3.0, 3.0) * 0.06
    rows_idx = jnp.arange(NB)[:, None]
    cols_idx = jnp.arange(NB)[None, :]
    upper = (cols_idx > rows_idx).astype(jnp.float32)
    eye_mat = (cols_idx == rows_idx).astype(jnp.float32)
    scale = 0.5 / jnp.sqrt(jnp.float32(NB) * jnp.float32(N))
    full = (off_vals * upper[None] + diag_vals[:, :, None] * eye_mat[None]) * scale
    return full.astype(jnp.bfloat16)


def level_of(key, extent, cuts, low, largest):
    level = 1.0
    for position, shards_of in cuts:
        heights = jax.random.uniform(jax.random.fold_in(jax.random.fold_in(key, 6), position), (shards_of,), jnp.float32, low / len(cuts), largest / len(cuts))
        level = level * jnp.repeat(jnp.exp(heights), extent[position] // shards_of).reshape((-1,) + (1,) * (len(extent) - 1 - position))
    return level


def gaussian(rng, dims, spread, limit, cuts=(), kind=jnp.bfloat16):
    gain = level_of(rng, dims, cuts, -0.22, 0.18) if cuts else 1.0
    drawn = jax.random.normal(rng, dims, jnp.float32) * spread * gain
    return jnp.minimum(jnp.maximum(drawn, -limit), limit).astype(kind)


def setup_inputs(seed: int = 0) -> dict:
    key_of = jax.random.split(jax.random.key(seed), 4)
    vectors = gaussian(key_of[0], (N, M), 1.0, 6.0, ((0, 128), (1, 2)), jnp.float32)
    reflectors = gaussian(key_of[1], (2, N, NB), 1.0, 6.0, ((0, 2), (1, 128)))
    factors = draw_factors(jax.random.fold_in(key_of[3], 71), 0)
    return {"vectors": vectors, "reflectors": reflectors, "factors": factors}


def reference(vectors, reflectors, factors):
    reflect = reflectors.astype(jnp.float32)
    triang = factors.astype(jnp.float32)
    current = vectors
    for which in (1, 0):
        summed = jnp.dot(reflect[which].T, current, precision=lax.Precision.HIGHEST)
        applied = jnp.dot(triang[which], summed, precision=lax.Precision.HIGHEST)
        current = current - jnp.dot(reflect[which], applied, precision=lax.Precision.HIGHEST)
    return current
```

```python
import functools

import jax
import jax.numpy as jnp
from jax import lax
from jax.experimental import pallas as pl
from jax.experimental.pallas import tpu as pltpu
from jax.sharding import PartitionSpec as P

MESH = pl.DeviceIdType.MESH
F32 = jnp.float32
BF16 = jnp.bfloat16
ROWS, COLS, NB = 1536, 1024, 128
TILE = 256
VLIM = 40
BLOCK = 256
JOBS = (
    ("own", 0, 128, 0, 512, False, False),
    ("own", 0, 128, 512, 512, False, False),
    ("other", 0, 64, 0, 1024, False, False),
    ("other", 64, 48, 0, 1024, False, False),
    ("other", 112, 16, 0, 1024, True, True),
)
OTHER = (2, 3, 4)
ORDER = (
    ("c", 0), ("c", 1), (1, 0), (1, 1), ("c", 2), (2, 0), (1, 2), ("c", 3), (2, 1), ("c", 4), (1, 3), (2, 2), (3, 0), (2, 3), (2, 4),
    (3, 1), (3, 2), (4, 0), (4, 1), (3, 3), (3, 4), (5, 0), (5, 1), ("f", 0), (4, 2), (5, 2), (4, 3), (5, 4), (5, 3),
)


def tiles_of(job):
    return job[2] // 8 * (job[4] // 128) + (16 if job[5] else 0)


def split(value):
    high = value.astype(BF16)
    return high, (value - high.astype(F32)).astype(BF16)


def dot(a, b):
    return jnp.dot(a, b, preferred_element_type=F32)


def dot3(a, b):
    ah, al = split(a)
    bh, bl = split(b)
    return dot(ah, bh) + dot(ah, bl) + dot(al, bh)


def dot2(a, b):
    bh, bl = split(b)
    return dot(a, bh) + dot(a, bl)


def reduce_kernel(x_hbm, v_hbm, t_hbm, xf, yh_ref, yl_ref, v_out, *scratch):
    (v_ref, t_ref, xh, xl, vt_own, vt_oth, t_oth, a_own, in_sem, v_send, v_recv, s_send, s_recv), bufs = scratch[:13], scratch[13:]
    per = [bufs[i * 5 : i * 5 + 5] for i in range(len(JOBS))]
    row = lax.axis_index("row")
    col = lax.axis_index("col")
    core = lax.rem(row, 2)
    x = lax.rem(row // 2, 4)
    z = lax.rem(row // 8, 8)
    y = row // 64
    place = x * 2 + y
    place16 = core * 8 + place

    def at(y, z, x, core):
        return {"row": ((y * 8 + z) * 4 + x) * 2 + core, "col": col}

    partner = {"row": row, "col": 1 - col}
    sibling = at(y, z, x, 1 - core)
    v_load = pltpu.make_async_copy(v_hbm.at[0], v_ref, in_sem.at[COLS // TILE])
    v_load.start()
    t_load = pltpu.make_async_copy(t_hbm.at[0], t_ref, in_sem.at[COLS // TILE + 1])
    t_load.start()
    loads = []
    for t in range(COLS // TILE):
        part = (slice(None), pl.ds(t * TILE, TILE))
        load = pltpu.make_async_copy(x_hbm.at[part], xf.at[part], in_sem.at[t])
        load.start()
        loads.append(load)

    barrier = pltpu.get_barrier_semaphore()
    peers = [partner, sibling]
    for k in range(1, 8):
        p = lax.rem(place + k, 8)
        peers += [at(lax.rem(p, 2), z, p // 2, c) for c in (core, 1 - core)]
    peers += [at(y, lax.rem(z + k, 8), x, core) for k in range(1, 8)]
    for peer in peers:
        pl.semaphore_signal(barrier, inc=1, device_id=peer, device_id_type=MESH)
    v_load.wait()
    vt_own[...] = v_ref[...].T
    t_load.wait()
    pl.semaphore_wait(barrier, len(peers))

    def remote(src, dst, send, recv, peer):
        return pltpu.make_async_remote_copy(
            src_ref=src, dst_ref=dst, send_sem=send, recv_sem=recv, device_id=peer, device_id_type=MESH
        )

    v_copies = []
    for i, job in enumerate(OTHER):
        part = pl.ds(JOBS[job][1], JOBS[job][2])
        v_copies.append(remote(vt_own.at[part], vt_oth.at[part], v_send.at[i], v_recv.at[i], partner))
    v_copies.append(remote(t_ref, t_oth, v_send.at[len(OTHER)], v_recv.at[len(OTHER)], partner))
    for copy in v_copies:
        copy.start()

    def drain(ref, count, sem):
        part = ref.at[pl.ds(0, count)]
        pltpu.make_async_copy(part, part, sem).wait()

    def compute(j):
        block, first, count, col0, cols, gram, both = JOBS[j]
        part_ref = per[j][0]
        r8 = count // 8
        if block == "other":
            v_copies[OTHER.index(j)].wait_recv()
        for t in range(col0 // TILE, (col0 + cols) // TILE):
            cs = pl.ds(t * TILE, TILE)
            if block == "own":
                loads[t].wait()
                high, low = split(xf[:, cs])
                xh[:, cs] = high
                xl[:, cs] = low
                lhs = vt_own[pl.ds(first, count), :]
            else:
                high, low = xh[:, cs], xl[:, cs]
                lhs = vt_oth[pl.ds(first, count), :]
            value = dot(lhs, high) + dot(lhs, low)
            for s in range(TILE // 128):
                base = ((t * TILE - col0) // 128 + s) * r8
                part_ref[pl.ds(base, r8)] = value[:, s * 128 : (s + 1) * 128].reshape(r8, 8, 128)
        if gram:
            value = dot(vt_oth[...], v_ref[...])
            part_ref[pl.ds(tiles_of(JOBS[j]) - 16, 16)] = value.reshape(16, 8, 128)
        half = tiles_of(JOBS[j]) // 2
        if both:
            q = half // 8
            rx = per[j][2]
            spread(j, 1, lambda p: (part_ref.at[pl.ds(p * q, q)], rx.at[pl.ds(place16 * q, q)]))
            rx[pl.ds(place16 * q, q)] = part_ref[pl.ds(place16 * q, q)]
        else:
            remote(part_ref.at[pl.ds((1 - core) * half, half)], per[j][1], s_send.at[j, 0], s_recv.at[j, 0], sibling).start()

    def spread(j, phase, refs):
        n = group(j)
        for k in range(1, n):
            p = lax.rem(place + k, 8)
            c = core if k < 8 else 1 - core
            src, dst = refs(c * 8 + p)
            remote(src, dst, s_send.at[j, phase], s_recv.at[j, phase], at(lax.rem(p, 2), z, p // 2, c)).start()

    def group(j):
        return 16 if JOBS[j][6] else 8

    def counts(j):
        n = tiles_of(JOBS[j])
        q = n // 16
        g = group(j)
        core_hop = 0 if g == 16 else n // 2
        return (core_hop, (g - 1) * q, 7 * q, (g - 1) * q, core_hop)

    def arrived(j, phase, ref):
        drain(ref, counts(j)[phase], s_recv.at[j, phase])

    def total_of(ref, slots, q):
        total = ref[pl.ds(0, q)]
        for k in range(1, slots):
            total = total + ref[pl.ds(k * q, q)]
        return total

    def stage1(j):
        part_ref, got, rx, rz, fin = per[j]
        half = tiles_of(JOBS[j]) // 2
        q = half // 8
        arrived(j, 0, got)
        got[...] = got[...] + part_ref[pl.ds(core * half, half)]
        spread(j, 1, lambda p: (got.at[pl.ds((p - core * 8) * q, q)], rx.at[pl.ds(place * q, q)]))
        rx[pl.ds(place * q, q)] = got[pl.ds(place * q, q)]

    def stage2(j):
        part_ref, got, rx, rz, fin = per[j]
        q = tiles_of(JOBS[j]) // 16
        arrived(j, 1, rx)
        slot = pl.ds(z * q, q)
        rz[slot] = total_of(rx, group(j), q)
        for k in range(1, 8):
            zz = lax.rem(z + k, 8)
            remote(rz.at[slot], rz.at[slot], s_send.at[j, 2], s_recv.at[j, 2], at(y, zz, x, core)).start()

    def stage3(j):
        part_ref, got, rx, rz, fin = per[j]
        q = tiles_of(JOBS[j]) // 16
        arrived(j, 2, rz)
        slot = pl.ds(place16 * q, q)
        fin[slot] = total_of(rz, 8, q)
        spread(j, 3, lambda p: (fin.at[slot], fin.at[slot]))

    def stage4(j):
        fin = per[j][4]
        half = tiles_of(JOBS[j]) // 2
        arrived(j, 3, fin)
        mine = pl.ds(core * half, half)
        remote(fin.at[mine], fin.at[mine], s_send.at[j, 4], s_recv.at[j, 4], sibling).start()

    def stage5(j):
        arrived(j, 3 if JOBS[j][6] else 4, per[j][4])

    def columns(jobs_of, t):
        pieces = []
        for s in range(TILE // 128):
            parts = []
            for j, k in jobs_of(t * (TILE // 128) + s):
                count = JOBS[j][2]
                parts.append(per[j][4][pl.ds(k * (count // 8), count // 8)].reshape(count, 128))
            pieces.append(parts[0] if len(parts) == 1 else jnp.concatenate(parts, axis=0))
        return jnp.concatenate(pieces, axis=1)

    def apply_own(_):
        for t in range(COLS // TILE):
            w_own = columns(lambda k: [(k // 4, k % 4)], t)
            a_own[:, pl.ds(t * TILE, TILE)] = dot2(t_ref[...], w_own)

    run = {"c": compute, 1: stage1, 2: stage2, 3: stage3, 4: stage4, 5: stage5, "f": apply_own}
    for stage, j in ORDER:
        run[stage](j)
        if (stage, j) == (1, 3):
            v_out[:, :NB] = v_ref[...]
            v_out[:, NB:] = vt_oth[...].T
            v_copies[len(OTHER)].wait_recv()

    first = col == 0
    last = JOBS[OTHER[-1]]
    gram = per[OTHER[-1]][4][pl.ds(tiles_of(last) - 16, 16)].reshape(NB, NB)
    gram = jnp.where(first, gram.T, gram)
    t_zero = jnp.where(first, t_ref[...].astype(F32), t_oth[...].astype(F32)).astype(BF16)
    mh, ml = split(dot2(t_zero, gram))
    for t in range(COLS // TILE):
        cs = pl.ds(t * TILE, TILE)
        own = a_own[:, cs]
        oth = dot2(t_oth[...], columns(lambda k: [(j, k) for j in OTHER], t))
        y_one = jnp.where(first, oth, own)
        yh, yl = split(y_one)
        y_zero = jnp.where(first, own, oth) - (dot(mh, yh) + dot(mh, yl) + dot(ml, yh))
        y_own = jnp.where(first, y_zero, y_one)
        y_oth = jnp.where(first, y_one, y_zero)
        for base, value in ((0, y_own), (NB, y_oth)):
            high, low = split(value)
            yh_ref[pl.ds(base, NB), cs] = high
            yl_ref[pl.ds(base, NB), cs] = low

    for copy in v_copies:
        copy.wait_send()
    for j in range(len(JOBS)):
        for phase, count in enumerate(counts(j)):
            if count:
                drain(per[j][0], count, s_send.at[j, phase])


def update_kernel(x_ref, v_ref, yh_ref, yl_ref, o_hbm, out, sem):
    copies = []
    for i in range(ROWS // BLOCK):
        part = pl.ds(i * BLOCK, BLOCK)
        v = v_ref[part, :]
        out[part, :] = x_ref[part, :] - (dot(v, yh_ref[...]) + dot(v, yl_ref[...]))
        copy = pltpu.make_async_copy(out.at[part], o_hbm.at[part], sem.at[i])
        copy.start()
        copies.append(copy)
    for copy in copies:
        copy.wait()


def body(vectors, reflectors, factors):
    vmem = pl.BlockSpec(memory_space=pltpu.VMEM)
    scratch = [
        pltpu.VMEM((ROWS, NB), BF16),
        pltpu.VMEM((NB, NB), BF16),
        pltpu.VMEM((ROWS, COLS), BF16),
        pltpu.VMEM((ROWS, COLS), BF16),
        pltpu.VMEM((NB, ROWS), BF16),
        pltpu.VMEM((NB, ROWS), BF16),
        pltpu.VMEM((NB, NB), BF16),
        pltpu.VMEM((NB, COLS), F32),
        pltpu.SemaphoreType.DMA((COLS // TILE + 2,)),
        pltpu.SemaphoreType.DMA((len(OTHER) + 1,)),
        pltpu.SemaphoreType.DMA((len(OTHER) + 1,)),
        pltpu.SemaphoreType.DMA((len(JOBS), 5)),
        pltpu.SemaphoreType.DMA((len(JOBS), 5)),
    ]
    for job in JOBS:
        n = tiles_of(job)
        for count in (n, n // 2, n if job[6] else n // 2, n // 2, n):
            scratch.append(pltpu.VMEM((count, 8, 128), F32))
    hbm = pl.BlockSpec(memory_space=pltpu.HBM)
    vectors, y_high, y_low, v_all = pl.pallas_call(
        reduce_kernel,
        out_shape=(
            pltpu.VMEM((ROWS, COLS), F32),
            pltpu.VMEM((2 * NB, COLS), BF16),
            pltpu.VMEM((2 * NB, COLS), BF16),
            pltpu.VMEM((ROWS, 2 * NB), BF16),
        ),
        in_specs=[hbm, hbm, hbm],
        out_specs=(vmem, vmem, vmem, vmem),
        scratch_shapes=scratch,
        compiler_params=pltpu.CompilerParams(collective_id=0, has_side_effects=True, vmem_limit_bytes=VLIM << 20),
        cost_estimate=pl.CostEstimate(flops=2 * ROWS * COLS * 256 * 2, bytes_accessed=ROWS * COLS * 4, transcendentals=0),
        name="reduce",
    )(*(pltpu.with_memory_space_constraint(a, pltpu.HBM) for a in (vectors, reflectors, factors)))
    return pl.pallas_call(
        update_kernel,
        out_shape=jax.ShapeDtypeStruct((ROWS, COLS), F32),
        in_specs=[vmem, vmem, vmem, vmem],
        out_specs=hbm,
        scratch_shapes=[pltpu.VMEM((ROWS, COLS), F32), pltpu.SemaphoreType.DMA((ROWS // BLOCK,))],
        cost_estimate=pl.CostEstimate(flops=2 * ROWS * COLS * 512, bytes_accessed=ROWS * COLS * 8, transcendentals=0),
        compiler_params=pltpu.CompilerParams(vmem_limit_bytes=24 << 20),
        name="update",
    )(vectors, v_all, y_high, y_low)


def solution(mesh):
    return jax.shard_map(
        body,
        mesh=mesh,
        in_specs=(P("row", "col"), P("col", "row", None), P("col", None, None)),
        out_specs=P("row", "col"),
        check_vma=False,
    )
```

```python
import functools

import jax
import jax.numpy as jnp
from jax import lax
from jax.experimental import pallas as pl
from jax.experimental.pallas import tpu as pltpu
from jax.sharding import PartitionSpec as P

MESH = pl.DeviceIdType.MESH
F32 = jnp.float32
BF16 = jnp.bfloat16
ROWS, COLS, NB = 1536, 1024, 128
TILE = 256
VLIM = 40
BLOCKS = ((0, 768), (768, 512), (1280, 256))
JOBS = (
    ("own", 0, 128, 0, 512, False, False),
    ("own", 0, 128, 512, 512, False, False),
    ("other", 0, 64, 0, 1024, False, False),
    ("other", 64, 48, 0, 1024, False, False),
    ("other", 112, 16, 0, 1024, True, True),
)
OWN = (0, 1)
OTHER = (2, 3, 4)
ORDER = (
    ("c", 0), ("c", 1), (1, 0), (1, 1), ("c", 2), (2, 0), (1, 2), ("c", 3), (2, 1), ("c", 4), (1, 3), (2, 2), (3, 0), (2, 3), (2, 4),
    (3, 1), (3, 2), (4, 0), (4, 1), (3, 3), (3, 4), (5, 0), (5, 1), ("f", 0), (4, 2), (5, 2), (4, 3), (5, 4), (5, 3),
)


PLANE = tuple(
    (dx, dy, dc)
    for dx, dy in ((2, 1), (1, 1), (3, 1), (2, 0), (1, 0), (3, 0), (0, 1), (0, 0))
    for dc in (1, 0)
    if dx or dy or dc
)
LINE = (4, 3, 5, 2, 6, 1, 7)


def tiles_of(job):
    return job[2] // 8 * (job[4] // 128) + (16 if job[5] else 0)


def split(value):
    high = value.astype(BF16)
    return high, (value - high.astype(F32)).astype(BF16)


def dot(a, b):
    return jnp.dot(a, b, preferred_element_type=F32)


def dot3(a, b):
    ah, al = split(a)
    bh, bl = split(b)
    return dot(ah, bh) + dot(ah, bl) + dot(al, bh)


def dot2(a, b):
    bh, bl = split(b)
    return dot(a, bh) + dot(a, bl)


def reduce_kernel(x_hbm, v_hbm, t_hbm, xf, yh_ref, yl_ref, v_out, *scratch):
    (v_ref, t_ref, xh, xl, vt_own, vt_oth, t_oth, a_own, in_sem, v_send, v_recv, s_send, s_recv), bufs = scratch[:13], scratch[13:]
    per = [bufs[i * 5 : i * 5 + 5] for i in range(len(JOBS))]
    row = lax.axis_index("row")
    col = lax.axis_index("col")
    core = lax.rem(row, 2)
    x = lax.rem(row // 2, 4)
    z = lax.rem(row // 8, 8)
    y = row // 64
    place = x * 2 + y
    place16 = core * 8 + place

    def at(y, z, x, core):
        return {"row": ((y * 8 + z) * 4 + x) * 2 + core, "col": col}

    partner = {"row": row, "col": 1 - col}
    sibling = at(y, z, x, 1 - core)
    v_load = pltpu.make_async_copy(v_hbm.at[0], v_ref, in_sem.at[COLS // TILE])
    v_load.start()
    barrier = pltpu.get_barrier_semaphore()
    peers = [at(lax.rem(y + dy, 2), z, lax.rem(x + dx, 4), lax.rem(core + dc, 2)) for dx, dy, dc in PLANE]
    peers.insert(4, partner)
    peers += [at(y, lax.rem(z + k, 8), x, core) for k in LINE]
    for peer in peers:
        pl.semaphore_signal(barrier, inc=1, device_id=peer, device_id_type=MESH)
    t_load = pltpu.make_async_copy(t_hbm.at[0], t_ref, in_sem.at[COLS // TILE + 1])
    t_load.start()
    loads = []
    for t in range(COLS // TILE):
        part = (slice(None), pl.ds(t * TILE, TILE))
        load = pltpu.make_async_copy(x_hbm.at[part], xf.at[part], in_sem.at[t])
        load.start()
        loads.append(load)
    v_load.wait()
    vt_own[...] = v_ref[...].T
    t_load.wait()
    pl.semaphore_wait(barrier, len(peers))

    def remote(src, dst, send, recv, peer):
        return pltpu.make_async_remote_copy(
            src_ref=src, dst_ref=dst, send_sem=send, recv_sem=recv, device_id=peer, device_id_type=MESH
        )

    v_copies = []
    for i, job in enumerate(OTHER):
        part = pl.ds(JOBS[job][1], JOBS[job][2])
        v_copies.append(remote(vt_own.at[part], vt_oth.at[part], v_send.at[i], v_recv.at[i], partner))
    v_copies.append(remote(t_ref, t_oth, v_send.at[len(OTHER)], v_recv.at[len(OTHER)], partner))
    for copy in v_copies:
        copy.start()

    def drain(ref, count, sem):
        part = ref.at[pl.ds(0, count)]
        pltpu.make_async_copy(part, part, sem).wait()

    def compute(j):
        block, first, count, col0, cols, gram, both = JOBS[j]
        part_ref = per[j][0]
        r8 = count // 8
        if block == "other":
            v_copies[OTHER.index(j)].wait_recv()
        for t in range(col0 // TILE, (col0 + cols) // TILE):
            cs = pl.ds(t * TILE, TILE)
            if block == "own":
                loads[t].wait()
                high, low = split(xf[:, cs])
                xh[:, cs] = high
                xl[:, cs] = low
                lhs = vt_own[pl.ds(first, count), :]
            else:
                high, low = xh[:, cs], xl[:, cs]
                lhs = vt_oth[pl.ds(first, count), :]
            value = dot(lhs, high) + dot(lhs, low)
            for s in range(TILE // 128):
                base = ((t * TILE - col0) // 128 + s) * r8
                part_ref[pl.ds(base, r8)] = value[:, s * 128 : (s + 1) * 128].reshape(r8, 8, 128)
        if gram:
            value = dot(vt_oth[...], v_ref[...])
            part_ref[pl.ds(tiles_of(JOBS[j]) - 16, 16)] = value.reshape(16, 8, 128)
        half = tiles_of(JOBS[j]) // 2
        if both:
            q = half // 8
            rx = per[j][2]
            spread(j, 1, lambda p: (part_ref.at[pl.ds(p * q, q)], rx.at[pl.ds(place16 * q, q)]))
            rx[pl.ds(place16 * q, q)] = part_ref[pl.ds(place16 * q, q)]
        else:
            remote(part_ref.at[pl.ds((1 - core) * half, half)], per[j][1], s_send.at[j, 0], s_recv.at[j, 0], sibling).start()

    def spread(j, phase, refs):
        for dx, dy, dc in PLANE:
            if dc and group(j) == 8:
                continue
            to = at(lax.rem(y + dy, 2), z, lax.rem(x + dx, 4), lax.rem(core + dc, 2))
            p = lax.rem(core + dc, 2) * 8 + lax.rem(x + dx, 4) * 2 + lax.rem(y + dy, 2)
            src, dst = refs(p)
            remote(src, dst, s_send.at[j, phase], s_recv.at[j, phase], to).start()

    def group(j):
        return 16 if JOBS[j][6] else 8

    def counts(j):
        n = tiles_of(JOBS[j])
        q = n // 16
        g = group(j)
        core_hop = 0 if g == 16 else n // 2
        return (core_hop, (g - 1) * q, 7 * q, (g - 1) * q, core_hop)

    def arrived(j, phase, ref):
        drain(ref, counts(j)[phase], s_recv.at[j, phase])

    def total_of(ref, slots, q):
        total = ref[pl.ds(0, q)]
        for k in range(1, slots):
            total = total + ref[pl.ds(k * q, q)]
        return total

    def stage1(j):
        part_ref, got, rx, rz, fin = per[j]
        half = tiles_of(JOBS[j]) // 2
        q = half // 8
        arrived(j, 0, got)
        got[...] = got[...] + part_ref[pl.ds(core * half, half)]
        spread(j, 1, lambda p: (got.at[pl.ds((p - core * 8) * q, q)], rx.at[pl.ds(place * q, q)]))
        rx[pl.ds(place * q, q)] = got[pl.ds(place * q, q)]

    def stage2(j):
        part_ref, got, rx, rz, fin = per[j]
        q = tiles_of(JOBS[j]) // 16
        arrived(j, 1, rx)
        slot = pl.ds(z * q, q)
        rz[slot] = total_of(rx, group(j), q)
        for k in LINE:
            zz = lax.rem(z + k, 8)
            remote(rz.at[slot], rz.at[slot], s_send.at[j, 2], s_recv.at[j, 2], at(y, zz, x, core)).start()

    def stage3(j):
        part_ref, got, rx, rz, fin = per[j]
        q = tiles_of(JOBS[j]) // 16
        arrived(j, 2, rz)
        slot = pl.ds(place16 * q, q)
        fin[slot] = total_of(rz, 8, q)
        spread(j, 3, lambda p: (fin.at[slot], fin.at[slot]))

    def stage4(j):
        fin = per[j][4]
        half = tiles_of(JOBS[j]) // 2
        arrived(j, 3, fin)
        mine = pl.ds(core * half, half)
        remote(fin.at[mine], fin.at[mine], s_send.at[j, 4], s_recv.at[j, 4], sibling).start()

    def stage5(j):
        arrived(j, 3 if JOBS[j][6] else 4, per[j][4])

    def columns(jobs_of, t):
        pieces = []
        for s in range(TILE // 128):
            parts = []
            for j, k in jobs_of(t * (TILE // 128) + s):
                count = JOBS[j][2]
                parts.append(per[j][4][pl.ds(k * (count // 8), count // 8)].reshape(count, 128))
            pieces.append(parts[0] if len(parts) == 1 else jnp.concatenate(parts, axis=0))
        return jnp.concatenate(pieces, axis=1)

    def apply_own(_):
        for t in range(COLS // TILE):
            w_own = columns(lambda k: [(j, k - JOBS[j][3] // 128) for j in OWN if 0 <= k * 128 - JOBS[j][3] < JOBS[j][4]], t)
            a_own[:, pl.ds(t * TILE, TILE)] = dot2(t_ref[...], w_own)

    run = {"c": compute, 1: stage1, 2: stage2, 3: stage3, 4: stage4, 5: stage5, "f": apply_own}
    for stage, j in ORDER:
        run[stage](j)
        if (stage, j) == ("c", OTHER[-1]):
            v_out[:, :NB] = v_ref[...]
            v_out[:, NB:] = vt_oth[...].T
            v_copies[len(OTHER)].wait_recv()

    first = col == 0
    last = JOBS[OTHER[-1]]
    gram = per[OTHER[-1]][4][pl.ds(tiles_of(last) - 16, 16)].reshape(NB, NB)
    gram = jnp.where(first, gram.T, gram)
    t_zero = jnp.where(first, t_ref[...].astype(F32), t_oth[...].astype(F32)).astype(BF16)
    mh, ml = split(dot2(t_zero, gram))
    for t in range(COLS // TILE):
        cs = pl.ds(t * TILE, TILE)
        own = a_own[:, cs]
        oth = dot2(t_oth[...], columns(lambda k: [(j, k) for j in OTHER], t))
        y_one = jnp.where(first, oth, own)
        yh, yl = split(y_one)
        y_zero = jnp.where(first, own, oth) - (dot(mh, yh) + dot(mh, yl) + dot(ml, yh))
        y_own = jnp.where(first, y_zero, y_one)
        y_oth = jnp.where(first, y_one, y_zero)
        for base, value in ((0, y_own), (NB, y_oth)):
            high, low = split(value)
            yh_ref[pl.ds(base, NB), cs] = high
            yl_ref[pl.ds(base, NB), cs] = low

    for copy in v_copies:
        copy.wait_send()
    for j in range(len(JOBS)):
        for phase, count in enumerate(counts(j)):
            if count:
                drain(per[j][0], count, s_send.at[j, phase])


def update_kernel(x_ref, v_ref, yh_ref, yl_ref, o_hbm, out, sem):
    copies = []
    for i, (first, count) in enumerate(BLOCKS):
        part = pl.ds(first, count)
        v = v_ref[part, :]
        out[part, :] = x_ref[part, :] - (dot(v, yh_ref[...]) + dot(v, yl_ref[...]))
        copy = pltpu.make_async_copy(out.at[part], o_hbm.at[part], sem.at[i])
        copy.start()
        copies.append(copy)
    for copy in copies:
        copy.wait()


def body(vectors, reflectors, factors):
    vmem = pl.BlockSpec(memory_space=pltpu.VMEM)
    scratch = [
        pltpu.VMEM((ROWS, NB), BF16),
        pltpu.VMEM((NB, NB), BF16),
        pltpu.VMEM((ROWS, COLS), BF16),
        pltpu.VMEM((ROWS, COLS), BF16),
        pltpu.VMEM((NB, ROWS), BF16),
        pltpu.VMEM((NB, ROWS), BF16),
        pltpu.VMEM((NB, NB), BF16),
        pltpu.VMEM((NB, COLS), F32),
        pltpu.SemaphoreType.DMA((COLS // TILE + 2,)),
        pltpu.SemaphoreType.DMA((len(OTHER) + 1,)),
        pltpu.SemaphoreType.DMA((len(OTHER) + 1,)),
        pltpu.SemaphoreType.DMA((len(JOBS), 5)),
        pltpu.SemaphoreType.DMA((len(JOBS), 5)),
    ]
    for job in JOBS:
        n = tiles_of(job)
        for count in (n, n // 2, n if job[6] else n // 2, n // 2, n):
            scratch.append(pltpu.VMEM((count, 8, 128), F32))
    hbm = pl.BlockSpec(memory_space=pltpu.HBM)
    vectors, y_high, y_low, v_all = pl.pallas_call(
        reduce_kernel,
        out_shape=(
            pltpu.VMEM((ROWS, COLS), F32),
            pltpu.VMEM((2 * NB, COLS), BF16),
            pltpu.VMEM((2 * NB, COLS), BF16),
            pltpu.VMEM((ROWS, 2 * NB), BF16),
        ),
        in_specs=[hbm, hbm, hbm],
        out_specs=(vmem, vmem, vmem, vmem),
        scratch_shapes=scratch,
        compiler_params=pltpu.CompilerParams(collective_id=0, has_side_effects=True, vmem_limit_bytes=VLIM << 20),
        cost_estimate=pl.CostEstimate(flops=2 * ROWS * COLS * 256 * 2, bytes_accessed=ROWS * COLS * 4, transcendentals=0),
        name="reduce",
    )(*(pltpu.with_memory_space_constraint(a, pltpu.HBM) for a in (vectors, reflectors, factors)))
    return pl.pallas_call(
        update_kernel,
        out_shape=jax.ShapeDtypeStruct((ROWS, COLS), F32),
        in_specs=[vmem, vmem, vmem, vmem],
        out_specs=hbm,
        scratch_shapes=[pltpu.VMEM((ROWS, COLS), F32), pltpu.SemaphoreType.DMA((len(BLOCKS),))],
        cost_estimate=pl.CostEstimate(flops=2 * ROWS * COLS * 512, bytes_accessed=ROWS * COLS * 8, transcendentals=0),
        compiler_params=pltpu.CompilerParams(vmem_limit_bytes=24 << 20),
        name="update",
    )(vectors, v_all, y_high, y_low)


def solution(mesh):
    return jax.shard_map(
        body,
        mesh=mesh,
        in_specs=(P("row", "col"), P("col", "row", None), P("col", None, None)),
        out_specs=P("row", "col"),
        check_vma=False,
    )
```

```python
import functools

import jax
import jax.numpy as jnp
from jax import lax
from jax.experimental import pallas as pl
from jax.experimental.pallas import tpu as pltpu
from jax.sharding import PartitionSpec as P

MESH = pl.DeviceIdType.MESH
F32 = jnp.float32
BF16 = jnp.bfloat16
ROWS, COLS, NB = 1536, 1024, 128
TILE = 256
VLIM = 40
BLOCKS = tuple((first, 256) for first in range(0, 1536, 256))
JOBS = (
    ("own", 0, 128, 0, 512, False, False),
    ("own", 0, 128, 512, 512, False, False),
    ("other", 0, 64, 0, 1024, False, False),
    ("other", 64, 48, 0, 1024, False, False),
    ("other", 112, 16, 0, 1024, True, True),
)
OWN = (0, 1)
OTHER = (2, 3, 4)
ORDER = (
    ("c", 0), ("c", 1), (1, 0), (1, 1), ("c", 2), (2, 0), (1, 2), ("c", 3), (2, 1), ("c", 4), (1, 3), (2, 2), (3, 0), (2, 3), (2, 4),
    ("v", 0), (3, 1), (3, 2), (4, 0), (4, 1), (3, 3), (3, 4), (5, 0), (5, 1), ("f", 0), (4, 2), (5, 2), (4, 3), (5, 4), ("g", 0), (5, 3),
)
PLANE = tuple(
    (dx, dy, dc)
    for dx, dy in ((2, 1), (1, 1), (3, 1), (2, 0), (1, 0), (3, 0), (0, 1), (0, 0))
    for dc in (1, 0)
    if dx or dy or dc
)
LINE = (4, 3, 5, 2, 6, 1, 7)


def tiles_of(job):
    return job[2] // 8 * (job[4] // 128) + (16 if job[5] else 0)


def split(value):
    high = value.astype(BF16)
    return high, (value - high.astype(F32)).astype(BF16)


def dot(a, b):
    return jnp.dot(a, b, preferred_element_type=F32)


def dot3(a, b):
    ah, al = split(a)
    bh, bl = split(b)
    return dot(ah, bh) + dot(ah, bl) + dot(al, bh)


def dot2(a, b):
    bh, bl = split(b)
    return dot(a, bh) + dot(a, bl)


def reduce_kernel(x_hbm, v_hbm, t_hbm, xf, yh_ref, yl_ref, v_out, *scratch):
    (v_ref, t_ref, xh, xl, vt_own, vt_oth, t_oth, a_own, m_ref, in_sem, v_send, v_recv, s_send, s_recv), bufs = scratch[:14], scratch[14:]
    per = [bufs[i * 5 : i * 5 + 5] for i in range(len(JOBS))]
    row = lax.axis_index("row")
    col = lax.axis_index("col")
    core = lax.rem(row, 2)
    x = lax.rem(row // 2, 4)
    z = lax.rem(row // 8, 8)
    y = row // 64
    place = x * 2 + y
    place16 = core * 8 + place

    def at(y, z, x, core):
        return {"row": ((y * 8 + z) * 4 + x) * 2 + core, "col": col}

    partner = {"row": row, "col": 1 - col}
    sibling = at(y, z, x, 1 - core)
    v_load = pltpu.make_async_copy(v_hbm.at[0], v_ref, in_sem.at[COLS // TILE])
    v_load.start()
    barrier = pltpu.get_barrier_semaphore()
    peers = [at(lax.rem(y + dy, 2), z, lax.rem(x + dx, 4), lax.rem(core + dc, 2)) for dx, dy, dc in PLANE]
    peers.insert(4, partner)
    peers += [at(y, lax.rem(z + k, 8), x, core) for k in LINE]
    for peer in peers:
        pl.semaphore_signal(barrier, inc=1, device_id=peer, device_id_type=MESH)
    t_load = pltpu.make_async_copy(t_hbm.at[0], t_ref, in_sem.at[COLS // TILE + 1])
    t_load.start()
    loads = []
    for t in range(COLS // TILE):
        part = (slice(None), pl.ds(t * TILE, TILE))
        load = pltpu.make_async_copy(x_hbm.at[part], xf.at[part], in_sem.at[t])
        load.start()
        loads.append(load)
    v_load.wait()
    vt_own[...] = v_ref[...].T
    t_load.wait()
    pl.semaphore_wait(barrier, len(peers))

    def remote(src, dst, send, recv, peer):
        return pltpu.make_async_remote_copy(
            src_ref=src, dst_ref=dst, send_sem=send, recv_sem=recv, device_id=peer, device_id_type=MESH
        )

    v_copies = []
    for i, job in enumerate(OTHER):
        part = pl.ds(JOBS[job][1], JOBS[job][2])
        v_copies.append(remote(vt_own.at[part], vt_oth.at[part], v_send.at[i], v_recv.at[i], partner))
    v_copies.append(remote(t_ref, t_oth, v_send.at[len(OTHER)], v_recv.at[len(OTHER)], partner))
    for copy in v_copies:
        copy.start()

    def drain(ref, count, sem):
        part = ref.at[pl.ds(0, count)]
        pltpu.make_async_copy(part, part, sem).wait()

    def compute(j):
        block, first, count, col0, cols, gram, both = JOBS[j]
        part_ref = per[j][0]
        r8 = count // 8
        if block == "other":
            v_copies[OTHER.index(j)].wait_recv()
        for t in range(col0 // TILE, (col0 + cols) // TILE):
            cs = pl.ds(t * TILE, TILE)
            if block == "own":
                loads[t].wait()
                high, low = split(xf[:, cs])
                xh[:, cs] = high
                xl[:, cs] = low
                lhs = vt_own[pl.ds(first, count), :]
            else:
                high, low = xh[:, cs], xl[:, cs]
                lhs = vt_oth[pl.ds(first, count), :]
            value = dot(lhs, high) + dot(lhs, low)
            for s in range(TILE // 128):
                base = ((t * TILE - col0) // 128 + s) * r8
                part_ref[pl.ds(base, r8)] = value[:, s * 128 : (s + 1) * 128].reshape(r8, 8, 128)
        if gram:
            value = dot(vt_oth[...], v_ref[...])
            part_ref[pl.ds(tiles_of(JOBS[j]) - 16, 16)] = value.reshape(16, 8, 128)
        half = tiles_of(JOBS[j]) // 2
        if both:
            q = half // 8
            rx = per[j][2]
            spread(j, 1, lambda p: (part_ref.at[pl.ds(p * q, q)], rx.at[pl.ds(place16 * q, q)]))
            rx[pl.ds(place16 * q, q)] = part_ref[pl.ds(place16 * q, q)]
        else:
            remote(part_ref.at[pl.ds((1 - core) * half, half)], per[j][1], s_send.at[j, 0], s_recv.at[j, 0], sibling).start()

    def spread(j, phase, refs):
        for dx, dy, dc in PLANE:
            if dc and group(j) == 8:
                continue
            to = at(lax.rem(y + dy, 2), z, lax.rem(x + dx, 4), lax.rem(core + dc, 2))
            p = lax.rem(core + dc, 2) * 8 + lax.rem(x + dx, 4) * 2 + lax.rem(y + dy, 2)
            src, dst = refs(p)
            remote(src, dst, s_send.at[j, phase], s_recv.at[j, phase], to).start()

    def group(j):
        return 16 if JOBS[j][6] else 8

    def counts(j):
        n = tiles_of(JOBS[j])
        q = n // 16
        g = group(j)
        core_hop = 0 if g == 16 else n // 2
        return (core_hop, (g - 1) * q, 7 * q, (g - 1) * q, core_hop)

    def arrived(j, phase, ref):
        drain(ref, counts(j)[phase], s_recv.at[j, phase])

    def total_of(ref, slots, q):
        total = ref[pl.ds(0, q)]
        for k in range(1, slots):
            total = total + ref[pl.ds(k * q, q)]
        return total

    def stage1(j):
        part_ref, got, rx, rz, fin = per[j]
        half = tiles_of(JOBS[j]) // 2
        q = half // 8
        arrived(j, 0, got)
        got[...] = got[...] + part_ref[pl.ds(core * half, half)]
        spread(j, 1, lambda p: (got.at[pl.ds((p - core * 8) * q, q)], rx.at[pl.ds(place * q, q)]))
        rx[pl.ds(place * q, q)] = got[pl.ds(place * q, q)]

    def stage2(j):
        part_ref, got, rx, rz, fin = per[j]
        q = tiles_of(JOBS[j]) // 16
        arrived(j, 1, rx)
        slot = pl.ds(z * q, q)
        rz[slot] = total_of(rx, group(j), q)
        for k in LINE:
            zz = lax.rem(z + k, 8)
            remote(rz.at[slot], rz.at[slot], s_send.at[j, 2], s_recv.at[j, 2], at(y, zz, x, core)).start()

    def stage3(j):
        part_ref, got, rx, rz, fin = per[j]
        q = tiles_of(JOBS[j]) // 16
        arrived(j, 2, rz)
        slot = pl.ds(place16 * q, q)
        fin[slot] = total_of(rz, 8, q)
        spread(j, 3, lambda p: (fin.at[slot], fin.at[slot]))

    def stage4(j):
        fin = per[j][4]
        half = tiles_of(JOBS[j]) // 2
        arrived(j, 3, fin)
        mine = pl.ds(core * half, half)
        remote(fin.at[mine], fin.at[mine], s_send.at[j, 4], s_recv.at[j, 4], sibling).start()

    def stage5(j):
        arrived(j, 3 if JOBS[j][6] else 4, per[j][4])

    def columns(jobs_of, t):
        pieces = []
        for s in range(TILE // 128):
            parts = []
            for j, k in jobs_of(t * (TILE // 128) + s):
                count = JOBS[j][2]
                parts.append(per[j][4][pl.ds(k * (count // 8), count // 8)].reshape(count, 128))
            pieces.append(parts[0] if len(parts) == 1 else jnp.concatenate(parts, axis=0))
        return jnp.concatenate(pieces, axis=1)

    def apply_own(_):
        for t in range(COLS // TILE):
            w_own = columns(lambda k: [(j, k - JOBS[j][3] // 128) for j in OWN if 0 <= k * 128 - JOBS[j][3] < JOBS[j][4]], t)
            a_own[:, pl.ds(t * TILE, TILE)] = dot2(t_ref[...], w_own)

    first = col == 0

    def hand_over(_):
        v_out[:, :NB] = v_ref[...]
        v_out[:, NB:] = vt_oth[...].T
        v_copies[len(OTHER)].wait_recv()

    def apply_gram(_):
        last = OTHER[-1]
        gram = per[last][4][pl.ds(tiles_of(JOBS[last]) - 16, 16)].reshape(NB, NB)
        gram = jnp.where(first, gram.T, gram)
        t_zero = jnp.where(first, t_ref[...].astype(F32), t_oth[...].astype(F32)).astype(BF16)
        m_ref[...] = dot2(t_zero, gram)

    run = {"v": hand_over, "g": apply_gram, "c": compute, 1: stage1, 2: stage2, 3: stage3, 4: stage4, 5: stage5, "f": apply_own}
    for stage, j in ORDER:
        run[stage](j)
    mh, ml = split(m_ref[...])
    for t in range(COLS // TILE):
        cs = pl.ds(t * TILE, TILE)
        own = a_own[:, cs]
        oth = dot2(t_oth[...], columns(lambda k: [(j, k) for j in OTHER], t))
        y_one = jnp.where(first, oth, own)
        yh, yl = split(y_one)
        y_zero = jnp.where(first, own, oth) - (dot(mh, yh) + dot(mh, yl) + dot(ml, yh))
        y_own = jnp.where(first, y_zero, y_one)
        y_oth = jnp.where(first, y_one, y_zero)
        for base, value in ((0, y_own), (NB, y_oth)):
            high, low = split(value)
            yh_ref[pl.ds(base, NB), cs] = high
            yl_ref[pl.ds(base, NB), cs] = low

    for copy in v_copies:
        copy.wait_send()
    for j in range(len(JOBS)):
        for phase, count in enumerate(counts(j)):
            if count:
                drain(per[j][0], count, s_send.at[j, phase])


def update_kernel(x_ref, v_ref, yh_ref, yl_ref, o_hbm, out, sem):
    copies = []
    for i, (first, count) in enumerate(BLOCKS):
        part = pl.ds(first, count)
        v = v_ref[part, :]
        out[part, :] = x_ref[part, :] - (dot(v, yh_ref[...]) + dot(v, yl_ref[...]))
        copy = pltpu.make_async_copy(out.at[part], o_hbm.at[part], sem.at[i])
        copy.start()
        copies.append(copy)
    for copy in copies:
        copy.wait()


def body(vectors, reflectors, factors):
    vmem = pl.BlockSpec(memory_space=pltpu.VMEM)
    scratch = [
        pltpu.VMEM((ROWS, NB), BF16),
        pltpu.VMEM((NB, NB), BF16),
        pltpu.VMEM((ROWS, COLS), BF16),
        pltpu.VMEM((ROWS, COLS), BF16),
        pltpu.VMEM((NB, ROWS), BF16),
        pltpu.VMEM((NB, ROWS), BF16),
        pltpu.VMEM((NB, NB), BF16),
        pltpu.VMEM((NB, COLS), F32),
        pltpu.VMEM((NB, NB), F32),
        pltpu.SemaphoreType.DMA((COLS // TILE + 2,)),
        pltpu.SemaphoreType.DMA((len(OTHER) + 1,)),
        pltpu.SemaphoreType.DMA((len(OTHER) + 1,)),
        pltpu.SemaphoreType.DMA((len(JOBS), 5)),
        pltpu.SemaphoreType.DMA((len(JOBS), 5)),
    ]
    for job in JOBS:
        n = tiles_of(job)
        for count in (n, n // 2, n if job[6] else n // 2, n // 2, n):
            scratch.append(pltpu.VMEM((count, 8, 128), F32))
    hbm = pl.BlockSpec(memory_space=pltpu.HBM)
    vectors, y_high, y_low, v_all = pl.pallas_call(
        reduce_kernel,
        out_shape=(
            pltpu.VMEM((ROWS, COLS), F32),
            pltpu.VMEM((2 * NB, COLS), BF16),
            pltpu.VMEM((2 * NB, COLS), BF16),
            pltpu.VMEM((ROWS, 2 * NB), BF16),
        ),
        in_specs=[hbm, hbm, hbm],
        out_specs=(vmem, vmem, vmem, vmem),
        scratch_shapes=scratch,
        compiler_params=pltpu.CompilerParams(collective_id=0, has_side_effects=True, vmem_limit_bytes=VLIM << 20),
        cost_estimate=pl.CostEstimate(flops=2 * ROWS * COLS * 256 * 2, bytes_accessed=ROWS * COLS * 4, transcendentals=0),
        name="reduce",
    )(*(pltpu.with_memory_space_constraint(a, pltpu.HBM) for a in (vectors, reflectors, factors)))
    return pl.pallas_call(
        update_kernel,
        out_shape=jax.ShapeDtypeStruct((ROWS, COLS), F32),
        in_specs=[vmem, vmem, vmem, vmem],
        out_specs=hbm,
        scratch_shapes=[pltpu.VMEM((ROWS, COLS), F32), pltpu.SemaphoreType.DMA((len(BLOCKS),))],
        cost_estimate=pl.CostEstimate(flops=2 * ROWS * COLS * 512, bytes_accessed=ROWS * COLS * 8, transcendentals=0),
        compiler_params=pltpu.CompilerParams(vmem_limit_bytes=24 << 20),
        name="update",
    )(vectors, v_all, y_high, y_low)


def solution(mesh):
    return jax.shard_map(
        body,
        mesh=mesh,
        in_specs=(P("row", "col"), P("col", "row", None), P("col", None, None)),
        out_specs=P("row", "col"),
        check_vma=False,
    )
```

```python
import functools

import jax
import jax.numpy as jnp
from jax import lax
from jax.experimental import pallas as pl
from jax.experimental.pallas import tpu as pltpu
from jax.sharding import PartitionSpec as P

MESH = pl.DeviceIdType.MESH
F32 = jnp.float32
BF16 = jnp.bfloat16
ROWS, COLS, NB = 1536, 1024, 128
TILE = 256
VLIM = 40
BLOCKS = tuple((first, 256) for first in range(0, 1536, 256))
JOBS = (
    ("own", 0, 128, 0, 512, False, False),
    ("own", 0, 128, 512, 512, False, False),
    ("other", 0, 64, 0, 1024, False, False),
    ("other", 64, 48, 0, 1024, False, False),
    ("other", 112, 16, 0, 1024, True, True),
)
OWN = (0, 1)
OTHER = (2, 3, 4)
ORDER = (
    ("c", 0), ("c", 1), (1, 0), (1, 1), ("c", 2), (2, 0), (1, 2), ("c", 3), (2, 1), ("c", 4), (1, 3), (2, 2), (3, 0), (2, 3), (2, 4),
    ("v", 0), (3, 1), (3, 2), (4, 0), (4, 1), (3, 3), (3, 4), (5, 0), (5, 1), (4, 2), (4, 3), ("f", 0), (5, 2), (5, 4), ("g", 0), (5, 3),
)
PLANE = tuple(
    (dx, dy, dc)
    for dx, dy in ((2, 1), (1, 1), (3, 1), (2, 0), (1, 0), (3, 0), (0, 1), (0, 0))
    for dc in (1, 0)
    if dx or dy or dc
)
LINE = (4, 3, 5, 2, 6, 1, 7)


def tiles_of(job):
    return job[2] // 8 * (job[4] // 128) + (16 if job[5] else 0)


def split(value):
    high = value.astype(BF16)
    return high, (value - high.astype(F32)).astype(BF16)


def dot(a, b):
    return jnp.dot(a, b, preferred_element_type=F32)


def dot3(a, b):
    ah, al = split(a)
    bh, bl = split(b)
    return dot(ah, bh) + dot(ah, bl) + dot(al, bh)


def dot2(a, b):
    bh, bl = split(b)
    return dot(a, bh) + dot(a, bl)


def reduce_kernel(x_hbm, v_hbm, t_hbm, xf, yh_ref, yl_ref, v_out, *scratch):
    (v_ref, t_ref, xh, xl, vt_own, vt_oth, t_oth, a_own, m_ref, in_sem, v_send, v_recv, s_send, s_recv), bufs = scratch[:14], scratch[14:]
    per = [bufs[i * 5 : i * 5 + 5] for i in range(len(JOBS))]
    row = lax.axis_index("row")
    col = lax.axis_index("col")
    core = lax.rem(row, 2)
    x = lax.rem(row // 2, 4)
    z = lax.rem(row // 8, 8)
    y = row // 64
    place = x * 2 + y
    place16 = core * 8 + place

    def at(y, z, x, core):
        return {"row": ((y * 8 + z) * 4 + x) * 2 + core, "col": col}

    partner = {"row": row, "col": 1 - col}
    sibling = at(y, z, x, 1 - core)
    v_load = pltpu.make_async_copy(v_hbm.at[0], v_ref, in_sem.at[COLS // TILE])
    v_load.start()
    barrier = pltpu.get_barrier_semaphore()
    peers = [at(lax.rem(y + dy, 2), z, lax.rem(x + dx, 4), lax.rem(core + dc, 2)) for dx, dy, dc in PLANE]
    peers.insert(4, partner)
    peers += [at(y, lax.rem(z + k, 8), x, core) for k in LINE]
    for peer in peers:
        pl.semaphore_signal(barrier, inc=1, device_id=peer, device_id_type=MESH)
    t_load = pltpu.make_async_copy(t_hbm.at[0], t_ref, in_sem.at[COLS // TILE + 1])
    t_load.start()
    loads = []
    for t in range(COLS // TILE):
        part = (slice(None), pl.ds(t * TILE, TILE))
        load = pltpu.make_async_copy(x_hbm.at[part], xf.at[part], in_sem.at[t])
        load.start()
        loads.append(load)
    v_load.wait()
    vt_own[...] = v_ref[...].T
    t_load.wait()
    pl.semaphore_wait(barrier, len(peers))

    def remote(src, dst, send, recv, peer):
        return pltpu.make_async_remote_copy(
            src_ref=src, dst_ref=dst, send_sem=send, recv_sem=recv, device_id=peer, device_id_type=MESH
        )

    v_copies = []
    for i, job in enumerate(OTHER):
        part = pl.ds(JOBS[job][1], JOBS[job][2])
        v_copies.append(remote(vt_own.at[part], vt_oth.at[part], v_send.at[i], v_recv.at[i], partner))
    v_copies.append(remote(t_ref, t_oth, v_send.at[len(OTHER)], v_recv.at[len(OTHER)], partner))
    for copy in v_copies:
        copy.start()

    def drain(ref, count, sem):
        part = ref.at[pl.ds(0, count)]
        pltpu.make_async_copy(part, part, sem).wait()

    def compute(j):
        block, first, count, col0, cols, gram, both = JOBS[j]
        part_ref = per[j][0]
        r8 = count // 8
        if block == "other":
            v_copies[OTHER.index(j)].wait_recv()
        for t in range(col0 // TILE, (col0 + cols) // TILE):
            cs = pl.ds(t * TILE, TILE)
            if block == "own":
                loads[t].wait()
                high, low = split(xf[:, cs])
                xh[:, cs] = high
                xl[:, cs] = low
                lhs = vt_own[pl.ds(first, count), :]
            else:
                high, low = xh[:, cs], xl[:, cs]
                lhs = vt_oth[pl.ds(first, count), :]
            value = dot(lhs, high) + dot(lhs, low)
            for s in range(TILE // 128):
                base = ((t * TILE - col0) // 128 + s) * r8
                part_ref[pl.ds(base, r8)] = value[:, s * 128 : (s + 1) * 128].reshape(r8, 8, 128)
        if gram:
            value = dot(vt_oth[...], v_ref[...])
            part_ref[pl.ds(tiles_of(JOBS[j]) - 16, 16)] = value.reshape(16, 8, 128)
        half = tiles_of(JOBS[j]) // 2
        if both:
            q = half // 8
            rx = per[j][2]
            spread(j, 1, lambda p: (part_ref.at[pl.ds(p * q, q)], rx.at[pl.ds(place16 * q, q)]))
            rx[pl.ds(place16 * q, q)] = part_ref[pl.ds(place16 * q, q)]
        else:
            remote(part_ref.at[pl.ds((1 - core) * half, half)], per[j][1], s_send.at[j, 0], s_recv.at[j, 0], sibling).start()

    def spread(j, phase, refs):
        for dx, dy, dc in PLANE:
            if dc and group(j) == 8:
                continue
            to = at(lax.rem(y + dy, 2), z, lax.rem(x + dx, 4), lax.rem(core + dc, 2))
            p = lax.rem(core + dc, 2) * 8 + lax.rem(x + dx, 4) * 2 + lax.rem(y + dy, 2)
            src, dst = refs(p)
            remote(src, dst, s_send.at[j, phase], s_recv.at[j, phase], to).start()

    def group(j):
        return 16 if JOBS[j][6] else 8

    def counts(j):
        n = tiles_of(JOBS[j])
        q = n // 16
        g = group(j)
        core_hop = 0 if g == 16 else n // 2
        return (core_hop, (g - 1) * q, 7 * q, (g - 1) * q, core_hop)

    def arrived(j, phase, ref):
        drain(ref, counts(j)[phase], s_recv.at[j, phase])

    def total_of(ref, slots, q):
        total = ref[pl.ds(0, q)]
        for k in range(1, slots):
            total = total + ref[pl.ds(k * q, q)]
        return total

    def stage1(j):
        part_ref, got, rx, rz, fin = per[j]
        half = tiles_of(JOBS[j]) // 2
        q = half // 8
        arrived(j, 0, got)
        got[...] = got[...] + part_ref[pl.ds(core * half, half)]
        spread(j, 1, lambda p: (got.at[pl.ds((p - core * 8) * q, q)], rx.at[pl.ds(place * q, q)]))
        rx[pl.ds(place * q, q)] = got[pl.ds(place * q, q)]

    def stage2(j):
        part_ref, got, rx, rz, fin = per[j]
        q = tiles_of(JOBS[j]) // 16
        arrived(j, 1, rx)
        slot = pl.ds(z * q, q)
        rz[slot] = total_of(rx, group(j), q)
        for k in LINE:
            zz = lax.rem(z + k, 8)
            remote(rz.at[slot], rz.at[slot], s_send.at[j, 2], s_recv.at[j, 2], at(y, zz, x, core)).start()

    def stage3(j):
        part_ref, got, rx, rz, fin = per[j]
        q = tiles_of(JOBS[j]) // 16
        arrived(j, 2, rz)
        slot = pl.ds(place16 * q, q)
        fin[slot] = total_of(rz, 8, q)
        spread(j, 3, lambda p: (fin.at[slot], fin.at[slot]))

    def stage4(j):
        fin = per[j][4]
        half = tiles_of(JOBS[j]) // 2
        arrived(j, 3, fin)
        mine = pl.ds(core * half, half)
        remote(fin.at[mine], fin.at[mine], s_send.at[j, 4], s_recv.at[j, 4], sibling).start()

    def stage5(j):
        arrived(j, 3 if JOBS[j][6] else 4, per[j][4])

    def columns(jobs_of, t):
        pieces = []
        for s in range(TILE // 128):
            parts = []
            for j, k in jobs_of(t * (TILE // 128) + s):
                count = JOBS[j][2]
                parts.append(per[j][4][pl.ds(k * (count // 8), count // 8)].reshape(count, 128))
            pieces.append(parts[0] if len(parts) == 1 else jnp.concatenate(parts, axis=0))
        return jnp.concatenate(pieces, axis=1)

    def apply_own(_):
        for t in range(COLS // TILE):
            w_own = columns(lambda k: [(j, k - JOBS[j][3] // 128) for j in OWN if 0 <= k * 128 - JOBS[j][3] < JOBS[j][4]], t)
            a_own[:, pl.ds(t * TILE, TILE)] = dot2(t_ref[...], w_own)

    first = col == 0

    def hand_over(_):
        v_out[:, :NB] = v_ref[...]
        v_out[:, NB:] = vt_oth[...].T
        v_copies[len(OTHER)].wait_recv()

    def apply_gram(_):
        last = OTHER[-1]
        gram = per[last][4][pl.ds(tiles_of(JOBS[last]) - 16, 16)].reshape(NB, NB)
        gram = jnp.where(first, gram.T, gram)
        t_zero = jnp.where(first, t_ref[...].astype(F32), t_oth[...].astype(F32)).astype(BF16)
        m_ref[...] = dot2(t_zero, gram)

    run = {"v": hand_over, "g": apply_gram, "c": compute, 1: stage1, 2: stage2, 3: stage3, 4: stage4, 5: stage5, "f": apply_own}
    for stage, j in ORDER:
        run[stage](j)
    mh, ml = split(m_ref[...])
    for t in range(COLS // TILE):
        cs = pl.ds(t * TILE, TILE)
        own = a_own[:, cs]
        oth = dot2(t_oth[...], columns(lambda k: [(j, k) for j in OTHER], t))
        y_one = jnp.where(first, oth, own)
        yh, yl = split(y_one)
        y_zero = jnp.where(first, own, oth) - (dot(mh, yh) + dot(mh, yl) + dot(ml, yh))
        y_own = jnp.where(first, y_zero, y_one)
        y_oth = jnp.where(first, y_one, y_zero)
        for base, value in ((0, y_own), (NB, y_oth)):
            high, low = split(value)
            yh_ref[pl.ds(base, NB), cs] = high
            yl_ref[pl.ds(base, NB), cs] = low

    for copy in v_copies:
        copy.wait_send()
    for j in range(len(JOBS)):
        for phase, count in enumerate(counts(j)):
            if count:
                drain(per[j][0], count, s_send.at[j, phase])


def update_kernel(x_ref, v_ref, yh_ref, yl_ref, o_hbm, out, sem):
    copies = []
    both = jnp.concatenate([yh_ref[...], yl_ref[...]], axis=0)
    for i, (first, count) in enumerate(BLOCKS):
        part = pl.ds(first, count)
        v = v_ref[part, :]
        out[part, :] = x_ref[part, :] - dot(jnp.concatenate([v, v], axis=1), both)
        copy = pltpu.make_async_copy(out.at[part], o_hbm.at[part], sem.at[i])
        copy.start()
        copies.append(copy)
    for copy in copies:
        copy.wait()


def body(vectors, reflectors, factors):
    vmem = pl.BlockSpec(memory_space=pltpu.VMEM)
    scratch = [
        pltpu.VMEM((ROWS, NB), BF16),
        pltpu.VMEM((NB, NB), BF16),
        pltpu.VMEM((ROWS, COLS), BF16),
        pltpu.VMEM((ROWS, COLS), BF16),
        pltpu.VMEM((NB, ROWS), BF16),
        pltpu.VMEM((NB, ROWS), BF16),
        pltpu.VMEM((NB, NB), BF16),
        pltpu.VMEM((NB, COLS), F32),
        pltpu.VMEM((NB, NB), F32),
        pltpu.SemaphoreType.DMA((COLS // TILE + 2,)),
        pltpu.SemaphoreType.DMA((len(OTHER) + 1,)),
        pltpu.SemaphoreType.DMA((len(OTHER) + 1,)),
        pltpu.SemaphoreType.DMA((len(JOBS), 5)),
        pltpu.SemaphoreType.DMA((len(JOBS), 5)),
    ]
    for job in JOBS:
        n = tiles_of(job)
        for count in (n, n // 2, n if job[6] else n // 2, n // 2, n):
            scratch.append(pltpu.VMEM((count, 8, 128), F32))
    hbm = pl.BlockSpec(memory_space=pltpu.HBM)
    vectors, y_high, y_low, v_all = pl.pallas_call(
        reduce_kernel,
        out_shape=(
            pltpu.VMEM((ROWS, COLS), F32),
            pltpu.VMEM((2 * NB, COLS), BF16),
            pltpu.VMEM((2 * NB, COLS), BF16),
            pltpu.VMEM((ROWS, 2 * NB), BF16),
        ),
        in_specs=[hbm, hbm, hbm],
        out_specs=(vmem, vmem, vmem, vmem),
        scratch_shapes=scratch,
        compiler_params=pltpu.CompilerParams(collective_id=0, has_side_effects=True, vmem_limit_bytes=VLIM << 20),
        cost_estimate=pl.CostEstimate(flops=2 * ROWS * COLS * 256 * 2, bytes_accessed=ROWS * COLS * 4, transcendentals=0),
        name="reduce",
    )(*(pltpu.with_memory_space_constraint(a, pltpu.HBM) for a in (vectors, reflectors, factors)))
    return pl.pallas_call(
        update_kernel,
        out_shape=jax.ShapeDtypeStruct((ROWS, COLS), F32),
        in_specs=[vmem, vmem, vmem, vmem],
        out_specs=hbm,
        scratch_shapes=[pltpu.VMEM((ROWS, COLS), F32), pltpu.SemaphoreType.DMA((len(BLOCKS),))],
        cost_estimate=pl.CostEstimate(flops=2 * ROWS * COLS * 512, bytes_accessed=ROWS * COLS * 8, transcendentals=0),
        compiler_params=pltpu.CompilerParams(vmem_limit_bytes=24 << 20),
        name="update",
    )(vectors, v_all, y_high, y_low)


def solution(mesh):
    return jax.shard_map(
        body,
        mesh=mesh,
        in_specs=(P("row", "col"), P("col", "row", None), P("col", None, None)),
        out_specs=P("row", "col"),
        check_vma=False,
    )
```
